32 devices in a mesh: tok: 8 (over y, x, core), blk: 4 (over z).
Axes of the slice: x: 2, y: 2, z: 4, core: 2. Of those that a mesh axis runs over, the one named last changes fastest.
Arguments:
- attn_out: bfloat16 [4096, 1536], P(('tok', 'blk')), may hold values from -6 to 6
- resid: bfloat16 [4096, 1536], P(('tok', 'blk')), may hold values from -6 to 6
- w_o: bfloat16 [1536, 1536], replicated, may hold values from -0.15625 to 0.15625
- norm1_gain: float32 [1536], replicated, may hold values from 0.1 to 1.9
- router_w: float32 [1536, 40], replicated, may hold values from -32 to 32
- route_slot: int32 [4096, 8], P(('tok', 'blk')), may hold values from 0 to 63, all different within a row; in each aligned block of 128 rows (0 to 127, 128 to 255, ...) at most 32 rows name the same one
- slot_expert: int32 [64], replicated, may hold values from 0 to 39, as said below
- keep: int32 [4096], P(('tok', 'blk')), may hold values 0 or 1
- w_gate: bfloat16 [64, 1536, 512], P('tok', 'blk'), may hold values from -0.15625 to 0.15625
- w_up: bfloat16 [64, 1536, 512], P('tok', 'blk'), may hold values from -0.15625 to 0.15625
- w_down: bfloat16 [64, 1536, 512], P('tok', 'blk'), may hold values from -0.25 to 0.25
- norm2_gain: float32 [1536], replicated, may hold values from 0.1 to 1.9
Outputs:
- layer_out: bfloat16 [4096, 1536], P(('tok', 'blk'))
The draws below stay inside these ranges and needn't reach their ends.
Inputs may be any that keep to these rules, and one draw needn't show every extreme that they name: `route_slot`: each row names 8 different slots; among the 128 rows of one device (aligned blocks of rows), no slot is named more than 32 times, a bound that some block reaches. `slot_expert`: every expert is named by one slot or more.
All inputs are finite; a program needn't handle non-finite values. No bound on the sum of `keep` on one device may be relied on, other than what follows from the above.
Results may differ from the reference program's by a relative error of at most 0.0099.
Values may be sent and summed in bfloat16 or wider, within the bound.
A program may use at most 128 MiB of HBM per device.

```python
import math
import jax
import jax.numpy as jnp
import numpy as np
from jax import lax

D = 1536
HD = 1536
FF = 512
EXPERTS = 40
TOP = 8
ROWS_DEV = 128
SLOTS = 64
CAP = 32
TOKENS = 4096


def draw_router_w(key, part):
    values = jax.random.normal(key, (D, EXPERTS), jnp.float32) * D ** (-0.5)
    return jnp.clip(values, -32.0, 32.0)


def draw_slot_expert(key, part):
    first = jax.random.permutation(jax.random.fold_in(key, 1), EXPERTS).astype(jnp.int32)
    extra = jax.random.randint(jax.random.fold_in(key, 2), (SLOTS - EXPERTS,), 0, EXPERTS).astype(jnp.int32)
    joined = jnp.concatenate([first, extra])
    return jax.random.permutation(jax.random.fold_in(key, 5), joined).astype(jnp.int32)


def with_ends(array, key, least, high):
    longest = array.shape.index(max(array.shape))
    spots = []
    for shift in (0, 1):
        where = [jax.random.randint(jax.random.fold_in(key, axis), (), 0, length) for axis, length in enumerate(array.shape)]
        where[longest] = (where[longest] + shift) % array.shape[longest]
        spots.append(tuple(where))
    return array.at[spots[0]].set(least).at[spots[1]].set(high)


def shard_levels(own_key, shape, shards, least, high):
    factor_of, own = 1.0, jax.random.fold_in(own_key, 6)
    for axis_at, parts in shards:
        steps = jnp.exp(jax.random.uniform(jax.random.fold_in(own, axis_at), (parts,), jnp.float32, least / len(shards), high / len(shards)))
        factor_of = factor_of * jnp.repeat(steps, shape[axis_at] // parts).reshape([-1 if axis == axis_at else 1 for axis in range(len(shape))])
    return factor_of


def routed_block(rng, own, number, rows, count, top, most, skew):
    sequence = jax.random.permutation(rng, count)
    crowded, ordinary = portions_of(count, rows * top, most, skew, True), portions_of(count, rows * top, most, skew, False)
    places = jnp.arange(count)

    def named(sizes, turn):
        used = int((sizes > 0).sum())
        fixed = max(1, used // 4)
        shifted = fixed + (places - fixed + turn * (used - fixed)) % max(1, count - fixed)
        return jnp.zeros((count,), jnp.int32).at[sequence[jnp.where(places < fixed, places, shifted)]].set(jnp.asarray(sizes, jnp.int32))

    sizes = jnp.where(number % 4 == 0, named(crowded, number // 4), named(ordinary, number - number // 4 - 1))
    mixed = jax.random.permutation(jax.random.fold_in(own, 3), count)
    donor, receiver = mixed[0:count // 2 * 2:2], mixed[1:count // 2 * 2:2]
    slack = jnp.minimum(sizes[donor] - 1, most - sizes[receiver]) // 2
    slack = jnp.where((donor == sequence[0]) | (receiver == sequence[0]) | (sizes[receiver] == 0), 0, jnp.maximum(slack, 0))
    shifted = jax.random.randint(jax.random.fold_in(own, 4), (count // 2,), 0, 1 << 20) % (slack + 1)
    sizes = sizes.at[donor].add(-shifted).at[receiver].add(shifted)
    items = jnp.searchsorted(jnp.cumsum(sizes), jnp.arange(rows * top), side="right").astype(jnp.int32)
    table = items.reshape(top, rows).T
    table = table[jax.random.permutation(jax.random.fold_in(own, 1), rows)]
    turn = jax.random.randint(jax.random.fold_in(own, 2), (rows, 1), 0, top)
    return jnp.take_along_axis(table, (jnp.arange(top)[None, :] + turn) % top, axis=1)


def portions_of(number_of, total, most, slope, full):
    portions = [(1 << 20) // math.isqrt(rank ** slope) + 1 for rank in range(1, number_of + 1)]
    largest = most if full else min(most, max(-(-total // number_of), total * portions[0] // sum(portions)))
    least = 1 if total - largest >= number_of - 1 else 0
    given, rest = [largest] + [least] * (number_of - 1), total - largest - least * (number_of - 1)
    while rest > 0:
        movable = [i for i in range(1, number_of) if given[i] < largest] or [i for i in range(1, number_of) if given[i] < most]
        whole, budget = sum([portions[i] for i in movable]), rest
        for i in movable:
            more = min(most - given[i], max(1, budget * portions[i] // whole), rest)
            given[i] = given[i] + more
            rest = rest - more
    return np.array(given)


def scatter_about(rng, dims, deviation, bound, cuts=(), held_as=jnp.bfloat16):
    drawn = jax.random.normal(rng, dims, jnp.float32) * deviation
    if len(cuts) > 0:
        drawn = shard_levels(rng, dims, cuts, -0.22, 0.18) * drawn
    return jnp.clip(drawn, min=-bound, max=bound).astype(held_as)


def setup_inputs(seed: int = 0) -> dict:
    arg_keys = jax.random.split(jax.random.key(seed), 13)
    attn_out = scatter_about(arg_keys[0], (TOKENS, HD), 1.0, 6.0, ((0, 32),))
    resid = scatter_about(arg_keys[1], (TOKENS, D), 1.0, 6.0, ((0, 32),))
    w_o = scatter_about(arg_keys[2], (HD, D), HD ** -0.5, 0.15625)
    norm1_gain = jnp.clip(1.0 + 0.18 * jax.random.normal(arg_keys[3], (D,), jnp.float32), 0.1, 1.9)
    router_w = draw_router_w(jax.random.fold_in(arg_keys[12], 71), 0)
    route_slot_keys = jax.random.split(jax.random.fold_in(arg_keys[5], 1), TOKENS // ROWS_DEV)
    route_slot_turns = jax.random.permutation(jax.random.fold_in(arg_keys[5], 3), TOKENS // ROWS_DEV)
    route_slot = jax.vmap(lambda own, number: routed_block(jax.random.fold_in(arg_keys[5], 2), own, number, ROWS_DEV, SLOTS, TOP, CAP, 2))(route_slot_keys, route_slot_turns).reshape((TOKENS, TOP))
    slot_expert = draw_slot_expert(jax.random.fold_in(arg_keys[12], 71), 0)
    keep = with_ends((jax.random.randint(arg_keys[7], (TOKENS,), 0, 8) < 7).astype(jnp.int32), jax.random.fold_in(arg_keys[7], 1), 0, 1)
    w_gate = scatter_about(arg_keys[8], (SLOTS, D, FF), D ** -0.5, 0.15625, ((0, 8), (1, 4)))
    w_up = scatter_about(arg_keys[9], (SLOTS, D, FF), D ** -0.5, 0.15625, ((0, 8), (1, 4)))
    w_down = scatter_about(arg_keys[10], (SLOTS, D, FF), FF ** -0.5, 0.25, ((0, 8), (1, 4)))
    norm2_gain = jnp.clip(1.0 + 0.18 * jax.random.normal(arg_keys[11], (D,), jnp.float32), 0.1, 1.9)
    return {"attn_out": attn_out, "resid": resid, "w_o": w_o, "norm1_gain": norm1_gain, "router_w": router_w, "route_slot": route_slot, "slot_expert": slot_expert, "keep": keep, "w_gate": w_gate, "w_up": w_up, "w_down": w_down, "norm2_gain": norm2_gain}


eps = 1e-05

def rms_scale(values, gain):
    mean_sq = lax.optimization_barrier(jnp.mean(values * values, axis=-1, keepdims=True))
    return values * lax.rsqrt(mean_sq + eps) * gain

def reference(attn_out, resid, w_o, norm1_gain, router_w, route_slot, slot_expert, keep, w_gate, w_up, w_down, norm2_gain):
    hidden_state = resid.astype(jnp.float32) + jnp.dot(attn_out, w_o, preferred_element_type=jnp.float32)
    normed = rms_scale(hidden_state, norm1_gain).astype(jnp.bfloat16)
    logits = jnp.dot(normed.astype(jnp.float32), router_w, precision=lax.Precision.HIGHEST)
    expert_of = slot_expert[route_slot]
    probs = jax.nn.softmax(jnp.take_along_axis(logits, expert_of, axis=1), axis=-1)
    live_rows = keep > 0
    weight = (probs * live_rows[:, None].astype(jnp.float32)).reshape(-1)
    flat_slot = route_slot.reshape(-1)
    live = jnp.repeat(live_rows, TOP)
    limit = CAP * (TOKENS // ROWS_DEV)

    def one_slot(total, slot):
        hit = (flat_slot == slot) & live
        index = jnp.nonzero(hit, size=limit, fill_value=0)[0]
        valid = jnp.arange(limit) < jnp.sum(hit.astype(jnp.int32))
        token_index = index // TOP
        rows = normed[token_index]
        gate = jnp.dot(rows, w_gate[slot], preferred_element_type=jnp.float32)
        up = jnp.dot(rows, w_up[slot], preferred_element_type=jnp.float32)
        act = (jax.nn.silu(gate) * up).astype(jnp.bfloat16)
        expert_y = jnp.dot(act, w_down[slot].T, preferred_element_type=jnp.float32).astype(jnp.bfloat16)
        scale = jnp.where(valid, weight[index], jnp.float32(0.0))
        total = total.at[token_index].add(scale[:, None] * expert_y.astype(jnp.float32))
        return (total, None)
    start = jnp.zeros(hidden_state.shape, jnp.float32)
    moe, unused = lax.scan(one_slot, start, jnp.arange(SLOTS, dtype=jnp.int32))
    mixed = hidden_state + moe
    return rms_scale(mixed, norm2_gain).astype(jnp.bfloat16)
```

```python
import jax
import jax.numpy as jnp
from jax import lax
from jax.sharding import PartitionSpec as P

eps = 1e-05


def rms_scale(values, gain):
    mean_sq = jnp.mean(values * values, axis=-1, keepdims=True)
    return values * lax.rsqrt(mean_sq + eps) * gain


def body(
    attn_out,
    resid,
    w_o,
    norm1_gain,
    router_w,
    route_slot,
    slot_expert,
    keep,
    w_gate,
    w_up,
    w_down,
    norm2_gain,
):
    rows, top = route_slot.shape
    width = resid.shape[1]
    slot_dev = w_gate.shape[0]
    groups = lax.axis_size("tok")
    slots = slot_dev * groups
    cap = max(2, 2 * rows * top // slots)
    hidden_state = resid.astype(jnp.float32) + jnp.dot(
        attn_out, w_o, preferred_element_type=jnp.float32
    )
    normed = rms_scale(hidden_state, norm1_gain).astype(jnp.bfloat16)
    logits = jnp.dot(normed.astype(jnp.float32), router_w, precision=lax.Precision.HIGHEST)
    slot_hits = route_slot[:, :, None] == jnp.arange(slots, dtype=jnp.int32)[None, None, :]
    expert_of = jnp.sum(jnp.where(slot_hits, slot_expert[None, None, :], 0), axis=-1)
    expert_hits = (
        expert_of[:, :, None] == jnp.arange(router_w.shape[1], dtype=jnp.int32)[None, None, :]
    )
    chosen = jnp.sum(jnp.where(expert_hits, logits[:, None, :], jnp.float32(0.0)), axis=-1)
    probs = jax.nn.softmax(chosen, axis=-1)
    live_rows = keep > 0
    live = jnp.repeat(live_rows, top)
    flat_hits = (slot_hits.reshape(rows * top, slots) & live[:, None]).astype(jnp.int32)
    before = jnp.cumsum(flat_hits, axis=0) - flat_hits
    position = jnp.sum(before * flat_hits, axis=1)
    flat_slot = route_slot.reshape(-1)
    owner = flat_slot // slot_dev
    local = flat_slot % slot_dev
    target_row = owner * cap + position
    target_local = jnp.where(live, local, slot_dev)
    token_index = jnp.arange(rows * top, dtype=jnp.int32) // top
    outgoing = jnp.zeros((slot_dev, groups * cap, width), jnp.bfloat16)
    outgoing = outgoing.at[target_local, target_row].set(normed[token_index], mode="drop")
    received = lax.all_to_all(outgoing, "tok", split_axis=1, concat_axis=1, tiled=True)
    gate_part = jnp.einsum(
        "snd,sdf->snf",
        received,
        lax.all_gather(w_gate, "blk", axis=1, tiled=True),
        preferred_element_type=jnp.float32,
    )
    up_part = jnp.einsum(
        "snd,sdf->snf",
        received,
        lax.all_gather(w_up, "blk", axis=1, tiled=True),
        preferred_element_type=jnp.float32,
    )
    act = (jax.nn.silu(gate_part) * up_part).astype(jnp.bfloat16)
    expert_y = jnp.einsum(
        "snf,sdf->snd",
        act,
        lax.all_gather(w_down, "blk", axis=1, tiled=True),
        preferred_element_type=jnp.float32,
    ).astype(jnp.bfloat16)
    returned = lax.all_to_all(expert_y, "tok", split_axis=1, concat_axis=1, tiled=True)
    picked = returned[local, target_row]
    scale = probs.reshape(-1) * live.astype(jnp.float32)
    moe = jnp.sum((picked.astype(jnp.float32) * scale[:, None]).reshape(rows, top, width), axis=1)
    mixed = hidden_state + moe
    return rms_scale(mixed, norm2_gain).astype(jnp.bfloat16)


def sparse_weight_plan(
    attn_out,
    resid,
    w_o,
    norm1_gain,
    router_w,
    route_slot,
    slot_expert,
    keep,
    w_gate,
    w_up,
    w_down,
    norm2_gain,
):
    rows = route_slot.shape[0]
    width = resid.shape[1]
    slot_dev, block, ff = w_gate.shape
    groups, blocks = lax.axis_size("tok"), lax.axis_size("blk")
    tok, blk = lax.axis_index("tok"), lax.axis_index("blk")
    slots = slot_dev * groups
    sub = slot_dev // blocks

    def to_block(sent, r):
        return lax.ppermute(sent, "blk", [(b, b ^ r) for b in range(blocks)]) if r else sent

    def share(w, r):
        return lax.dynamic_slice_in_dim(w, (blk ^ r) * sub, sub, axis=0)

    gate_up = [
        to_block(jnp.stack([share(w_gate, r), share(w_up, r)], axis=0), r) for r in range(blocks)
    ]
    held, w_down_late = lax.optimization_barrier((gate_up, w_down))
    gate_up = held
    down = [to_block(share(w_down_late, r), r) for r in range(blocks)]

    hidden_state = resid.astype(jnp.float32) + jnp.dot(
        attn_out, w_o, preferred_element_type=jnp.float32
    )
    normed = rms_scale(hidden_state, norm1_gain).astype(jnp.bfloat16)
    expert_pick = slot_expert[None, :] == jnp.arange(router_w.shape[1], dtype=jnp.int32)[:, None]
    logits = jnp.dot(normed.astype(jnp.float32), router_w, precision=lax.Precision.HIGHEST)
    slot_logits = jnp.sum(jnp.where(expert_pick[None], logits[:, :, None], 0.0), axis=1)
    hits = jnp.any(
        route_slot[:, :, None] == jnp.arange(slots, dtype=jnp.int32)[None, None, :], axis=1
    )
    top_logit = jnp.max(jnp.where(hits, slot_logits, -jnp.inf), axis=1, keepdims=True)
    powers = jnp.where(hits, jnp.exp(jnp.where(hits, slot_logits, top_logit) - top_logit), 0.0)
    probs = powers / jnp.sum(powers, axis=1, keepdims=True)
    probs = jnp.where((keep > 0)[:, None], probs, 0.0)
    high = lax.reduce_precision(probs, 8, 7)
    low = probs - high
    sent = jnp.concatenate(
        [normed, high.astype(jnp.bfloat16), low.astype(jnp.bfloat16)], axis=1
    )
    sent = lax.all_gather(sent, "blk", axis=0, tiled=True)
    sent = lax.all_gather(sent, "tok", axis=0, tiled=True)
    tokens = sent[:, :width]
    first = tok * slot_dev + blk * sub
    scale = lax.dynamic_slice_in_dim(sent, width + first, sub, axis=1).astype(
        jnp.float32
    ) + lax.dynamic_slice_in_dim(sent, width + slots + first, sub, axis=1).astype(jnp.float32)

    w_all = jnp.zeros((2, sub, width, ff), jnp.bfloat16)
    for r in range(blocks):
        w_all = lax.dynamic_update_slice_in_dim(w_all, gate_up[r], (blk ^ r) * block, axis=2)
    acts = []
    for s in range(sub):
        gate = jnp.dot(tokens, w_all[0, s], preferred_element_type=jnp.float32)
        up = jnp.dot(tokens, w_all[1, s], preferred_element_type=jnp.float32)
        acts.append((jax.nn.silu(gate) * up * scale[:, s : s + 1]).astype(jnp.bfloat16))
    act = jnp.concatenate(acts, axis=1)

    bits = []
    while 1 << len(bits) < groups:
        bits.append(len(bits))
    pieces = []
    for r in range(blocks):
        w = down[r].transpose(1, 0, 2).reshape(block, sub * ff)
        part = lax.dot_general(
            act, w, (((1,), (1,)), ((), ())), preferred_element_type=jnp.float32
        ).astype(jnp.bfloat16)
        part = part.reshape((2,) * len(bits) + (blocks * rows, block))
        order = bits[:1] + (bits[1:] if r % 2 == 0 else bits[1:][::-1])
        done = []
        for bit in order:
            axis = len(bits) - 1 - bit - sum(1 for d in done if d > bit)
            mine = (tok >> bit) & 1
            own = lax.dynamic_index_in_dim(part, mine, axis, keepdims=False)
            other = lax.dynamic_index_in_dim(part, 1 - mine, axis, keepdims=False)
            got = lax.ppermute(other, "tok", [(g, g ^ (1 << bit)) for g in range(groups)])
            part = (own.astype(jnp.float32) + got.astype(jnp.float32)).astype(jnp.bfloat16)
            done.append(bit)
        pieces.append(part)
    total = jnp.zeros((blocks * rows, width), jnp.bfloat16)
    for r in range(blocks):
        total = lax.dynamic_update_slice_in_dim(total, pieces[r], (blk ^ r) * block, axis=1)
    moe = jnp.zeros((rows, width), jnp.float32)
    for r in range(blocks):
        part = lax.dynamic_slice_in_dim(total, (blk ^ r) * rows, rows, axis=0)
        moe = moe + to_block(part, r).astype(jnp.float32)
    mixed = hidden_state + moe
    return rms_scale(mixed, norm2_gain).astype(jnp.bfloat16)


def solution(mesh):
    placed = (
        P(("tok", "blk"), None),
        P(("tok", "blk"), None),
        P(),
        P(),
        P(),
        P(("tok", "blk"), None),
        P(),
        P(("tok", "blk")),
        P("tok", "blk", None),
        P("tok", "blk", None),
        P("tok", "blk", None),
        P(),
    )
    groups, blocks = mesh.shape["tok"], mesh.shape["blk"]

    def layer(*args):
        split = args[8].shape[0] // groups % blocks == 0
        powers = groups & (groups - 1) == 0 and blocks & (blocks - 1) == 0
        plan = sparse_weight_plan if split and powers else body
        return jax.shard_map(
            plan,
            mesh=mesh,
            in_specs=placed,
            out_specs=P(("tok", "blk"), None),
            check_vma=False,
        )(*args)

    return layer
```

```python
import functools

import jax
import jax.numpy as jnp
from jax import lax
from jax.experimental import pallas as pl
from jax.experimental.pallas import tpu as pltpu
from jax.sharding import PartitionSpec as P

eps = 1e-05


def rms_scale(values, gain):
    mean_sq = jnp.mean(values * values, axis=-1, keepdims=True)
    return values * lax.rsqrt(mean_sq + eps) * gain


def body(
    attn_out,
    resid,
    w_o,
    norm1_gain,
    router_w,
    route_slot,
    slot_expert,
    keep,
    w_gate,
    w_up,
    w_down,
    norm2_gain,
):
    rows, top = route_slot.shape
    width = resid.shape[1]
    slot_dev = w_gate.shape[0]
    groups = lax.axis_size("tok")
    slots = slot_dev * groups
    cap = max(2, 2 * rows * top // slots)
    hidden_state = resid.astype(jnp.float32) + jnp.dot(
        attn_out, w_o, preferred_element_type=jnp.float32
    )
    normed = rms_scale(hidden_state, norm1_gain).astype(jnp.bfloat16)
    logits = jnp.dot(normed.astype(jnp.float32), router_w, precision=lax.Precision.HIGHEST)
    slot_hits = route_slot[:, :, None] == jnp.arange(slots, dtype=jnp.int32)[None, None, :]
    expert_of = jnp.sum(jnp.where(slot_hits, slot_expert[None, None, :], 0), axis=-1)
    expert_hits = (
        expert_of[:, :, None] == jnp.arange(router_w.shape[1], dtype=jnp.int32)[None, None, :]
    )
    chosen = jnp.sum(jnp.where(expert_hits, logits[:, None, :], jnp.float32(0.0)), axis=-1)
    probs = jax.nn.softmax(chosen, axis=-1)
    live_rows = keep > 0
    live = jnp.repeat(live_rows, top)
    flat_hits = (slot_hits.reshape(rows * top, slots) & live[:, None]).astype(jnp.int32)
    before = jnp.cumsum(flat_hits, axis=0) - flat_hits
    position = jnp.sum(before * flat_hits, axis=1)
    flat_slot = route_slot.reshape(-1)
    owner = flat_slot // slot_dev
    local = flat_slot % slot_dev
    target_row = owner * cap + position
    target_local = jnp.where(live, local, slot_dev)
    token_index = jnp.arange(rows * top, dtype=jnp.int32) // top
    outgoing = jnp.zeros((slot_dev, groups * cap, width), jnp.bfloat16)
    outgoing = outgoing.at[target_local, target_row].set(normed[token_index], mode="drop")
    received = lax.all_to_all(outgoing, "tok", split_axis=1, concat_axis=1, tiled=True)
    gate_part = jnp.einsum(
        "snd,sdf->snf",
        received,
        lax.all_gather(w_gate, "blk", axis=1, tiled=True),
        preferred_element_type=jnp.float32,
    )
    up_part = jnp.einsum(
        "snd,sdf->snf",
        received,
        lax.all_gather(w_up, "blk", axis=1, tiled=True),
        preferred_element_type=jnp.float32,
    )
    act = (jax.nn.silu(gate_part) * up_part).astype(jnp.bfloat16)
    expert_y = jnp.einsum(
        "snf,sdf->snd",
        act,
        lax.all_gather(w_down, "blk", axis=1, tiled=True),
        preferred_element_type=jnp.float32,
    ).astype(jnp.bfloat16)
    returned = lax.all_to_all(expert_y, "tok", split_axis=1, concat_axis=1, tiled=True)
    picked = returned[local, target_row]
    scale = probs.reshape(-1) * live.astype(jnp.float32)
    moe = jnp.sum((picked.astype(jnp.float32) * scale[:, None]).reshape(rows, top, width), axis=1)
    mixed = hidden_state + moe
    return rms_scale(mixed, norm2_gain).astype(jnp.bfloat16)


def flip(value, step):
    return value + step * (1 - 2 * ((value // step) % 2))


def turned(value, r):
    value = flip(value, 1) if r & 1 else value
    return flip(value, 2) if r & 2 else value


def expert_kernel(
    first_width,
    sent_ref,
    wg_ref,
    wu_ref,
    wd_ref,
    out_ref,
    tokens,
    gates,
    ups,
    downs,
    acts,
    sums,
    from_core,
    from_far,
    from_near,
    from_blk,
    send_sem,
    recv_sem,
    own_sem,
):
    a, b = lax.axis_index("tok"), lax.axis_index("blk")
    a_core, a_x, a_y = flip(a, 1), flip(a, 2), flip(a, 4)
    core, mx, my = a % 2, (a // 2) % 2, a // 4
    far = flip(a_x, 4)
    rows = sent_ref.shape[0]
    half = rows // 2
    sub = gates.shape[0]
    block = downs.shape[2]
    ff = gates.shape[2]
    number = iter(range(send_sem.shape[0]))
    started = []

    def send(src, dst, device):
        k = next(number)
        copy = pltpu.make_async_remote_copy(
            src_ref=src,
            dst_ref=dst,
            send_sem=send_sem.at[k],
            recv_sem=recv_sem.at[k],
            device_id=device,
            device_id_type=pl.DeviceIdType.MESH,
        )
        copy.start()
        started.append(copy)
        return copy

    barrier = pltpu.get_barrier_semaphore()
    partners = [(a_core, b), (a_x, b), (a_y, b)] + [(a, turned(b, r)) for r in (1, 2, 3)]
    for partner in partners:
        pl.semaphore_signal(
            barrier, inc=1, device_id=partner, device_id_type=pl.DeviceIdType.MESH
        )
    pl.semaphore_wait(barrier, len(partners))

    own = a * 4 + b
    tokens[own] = sent_ref[...]
    by_blk = {r: send(tokens.at[own], tokens.at[own], (a, turned(b, r))) for r in (1, 2, 3)}
    here = pl.ds(pl.multiple_of(b * block, 128), block)
    mine = [
        pltpu.make_async_copy(wg_ref.at[pl.ds(b * sub, sub)], gates.at[:, here], own_sem.at[0]),
        pltpu.make_async_copy(wu_ref.at[pl.ds(b * sub, sub)], ups.at[:, here], own_sem.at[1]),
        pltpu.make_async_copy(wd_ref.at[pl.ds(b * sub, sub)], downs.at[b], own_sem.at[2]),
    ]
    for copy in mine:
        copy.start()
    weights = []
    for r in (3, 2, 1):
        to = turned(b, r)
        part = pl.ds(to * sub, sub)
        weights.append(send(wg_ref.at[part], gates.at[:, here], (a, to)))
        weights.append(send(wu_ref.at[part], ups.at[:, here], (a, to)))

    def block_at(group, r):
        return tokens.at[group * 4 + turned(b, r)]

    def pass_on(group, r, to):
        return send(block_at(group, r), block_at(group, r), (to, b))

    by_x, by_y, by_core = {}, {}, []
    for r in range(4):
        if r:
            by_blk[r].wait_recv()
        by_x[r] = pass_on(a, r, a_x)
        by_y[r] = pass_on(a, r, a_y)
        by_core.append(pass_on(a, r, a_core))
    far_y, far_x = {}, {}
    for r in range(4):
        by_x[r].wait_recv()
        piece = tokens.at[a_x * 4 + turned(b, r), pl.ds(0, half)]
        far_y[r] = send(piece, piece, (a_y, b))
        by_core.append(pass_on(a_x, r, a_core))
        by_y[r].wait_recv()
        piece = tokens.at[a_y * 4 + turned(b, r), pl.ds(half, half)]
        far_x[r] = send(piece, piece, (a_x, b))
        by_core.append(pass_on(a_y, r, a_core))
    for r in range(4):
        far_y[r].wait_recv()
        far_x[r].wait_recv()
        by_core.append(pass_on(far, r, a_core))
    for copy in by_core:
        copy.wait_recv()

    for copy in weights:
        copy.wait_recv()
    for copy in mine:
        copy.wait()
    later = {}
    for r in (1, 3, 2):
        to = turned(b, r)
        later[r] = send(wd_ref.at[pl.ds(to * sub, sub)], downs.at[b], (a, to))

    width = gates.shape[1]
    tile = 4 * rows
    first = first_width * a + sub * b
    lanes = tokens.shape[2] - width
    lane = lax.broadcasted_iota(jnp.int32, (tile, lanes), 1)

    def expert_rows(t, carry):
        x = tokens[pl.ds(t * 4, 4)].reshape(tile, tokens.shape[2])
        parts = x[:, width:].astype(jnp.float32)
        x = x[:, :width]
        for s in range(sub):
            at = (lane == first + s) | (lane == first + s + lanes // 2)
            scale = jnp.sum(jnp.where(at, parts, 0.0), axis=1, keepdims=True)
            gate = jnp.dot(x, gates[s], preferred_element_type=jnp.float32)
            up = jnp.dot(x, ups[s], preferred_element_type=jnp.float32)
            act = gate / (1.0 + jnp.exp(-gate)) * up * scale
            acts[t, :, s * ff : (s + 1) * ff] = act.astype(jnp.bfloat16)
        return carry

    lax.fori_loop(0, 8, expert_rows, 0)

    def weighted(r):
        column = turned(b, r)

        def down_rows(t, carry):
            y = jnp.zeros((tile, block), jnp.float32)
            for s in range(sub):
                y = y + lax.dot_general(
                    acts[t, :, s * ff : (s + 1) * ff],
                    downs[column, s],
                    (((1,), (1,)), ((), ())),
                    preferred_element_type=jnp.float32,
                )
            sums[r, t % 2, t // 4, (t // 2) % 2] = y.astype(jnp.bfloat16)
            return carry

        if r:
            later[r].wait_recv()
        lax.fori_loop(0, 8, down_rows, 0)

    def add(r, i, j, got):
        sums[r, core, i, j] = (
            sums[r, core, i, j].astype(jnp.float32) + got.astype(jnp.float32)
        ).astype(jnp.bfloat16)

    step = [{}, {}, {}, {}]

    def send_core(r):
        step[0][r] = send(sums.at[r, 1 - core], from_core.at[r], (a_core, b))

    def send_far(r):
        step[0][r].wait_recv()
        for i in range(2):
            for j in range(2):
                add(r, i, j, from_core[r, i, j])
        if r % 2 == 0:
            step[1][r] = send(sums.at[r, core, :, 1 - mx], from_far.at[r], (a_x, b))
        else:
            step[1][r] = send(sums.at[r, core, 1 - my], from_far.at[r], (a_y, b))

    def send_near(r):
        step[1][r].wait_recv()
        for i in range(2):
            if r % 2 == 0:
                add(r, i, mx, from_far[r, i])
            else:
                add(r, my, i, from_far[r, i])
        if r % 2 == 0:
            step[2][r] = send(sums.at[r, core, 1 - my, mx], from_near.at[r], (a_y, b))
        else:
            step[2][r] = send(sums.at[r, core, my, 1 - mx], from_near.at[r], (a_x, b))

    def send_blk(r):
        step[2][r].wait_recv()
        add(r, my, mx, from_near[r])
        columns = pl.ds(pl.multiple_of(turned(b, r) * block, 128), block)
        for q in (3, 2, 1):
            to = turned(b, q)
            piece = pl.ds(pl.multiple_of(to * rows, 16), rows)
            step[3][r, q] = send(
                sums.at[r, core, my, mx, piece], from_blk.at[q - 1, :, columns], (a, to)
            )
        kept = sums[r, core, my, mx, pl.ds(pl.multiple_of(b * rows, 16), rows)]
        out_ref[:, columns] = kept.astype(jnp.float32)

    for r, n in ((0, 0), (1, 1), (3, 2), (2, 3)):
        weighted(r)
        send_core(r)
        if n >= 1:
            send_far((0, 1, 3)[n - 1])
    send_near(0)
    send_far(2)
    send_near(1)
    send_blk(0)
    send_near(3)
    send_blk(1)
    send_near(2)
    send_blk(3)
    send_blk(2)
    for copy in step[3].values():
        copy.wait_recv()
    out_ref[...] += (
        from_blk[0].astype(jnp.float32)
        + from_blk[1].astype(jnp.float32)
        + from_blk[2].astype(jnp.float32)
    )
    for copy in started:
        copy.wait_send()


def expert_sum(sent, w_gate, w_up, w_down):
    rows, sent_width = sent.shape
    slot_dev, block, ff = w_gate.shape
    sub = slot_dev // 4
    width = 4 * block
    tile = 4 * rows
    copies = 3 + 6 + 12 + 16 + 4 + 3 + 12 + 12
    bf16 = jnp.bfloat16
    macs = 32 * rows * sub * ff * width * 3
    return pl.pallas_call(
        functools.partial(expert_kernel, slot_dev),
        out_shape=jax.ShapeDtypeStruct((rows, width), jnp.float32),
        in_specs=[pl.BlockSpec(memory_space=pltpu.VMEM)]
        + [pl.BlockSpec(memory_space=pl.ANY)] * 3,
        out_specs=pl.BlockSpec(memory_space=pltpu.VMEM),
        scratch_shapes=[
            pltpu.VMEM((32, rows, sent_width), bf16),
            pltpu.VMEM((sub, width, ff), bf16),
            pltpu.VMEM((sub, width, ff), bf16),
            pltpu.VMEM((4, sub, block, ff), bf16),
            pltpu.VMEM((8, tile, sub * ff), bf16),
            pltpu.VMEM((4, 2, 2, 2, tile, block), bf16),
            pltpu.VMEM((4, 2, 2, tile, block), bf16),
            pltpu.VMEM((4, 2, tile, block), bf16),
            pltpu.VMEM((4, tile, block), bf16),
            pltpu.VMEM((3, rows, width), bf16),
            pltpu.SemaphoreType.DMA((copies,)),
            pltpu.SemaphoreType.DMA((copies,)),
            pltpu.SemaphoreType.DMA((3,)),
        ],
        compiler_params=pltpu.CompilerParams(
            collective_id=0, has_side_effects=True, vmem_limit_bytes=63 * 1024 * 1024
        ),
        cost_estimate=pl.CostEstimate(
            flops=2 * macs, bytes_accessed=3 * slot_dev * block * ff * 2, transcendentals=0
        ),
    )(sent, w_gate, w_up, w_down)


def whole_slot_plan(
    attn_out,
    resid,
    w_o,
    norm1_gain,
    router_w,
    route_slot,
    slot_expert,
    keep,
    w_gate,
    w_up,
    w_down,
    norm2_gain,
):
    rows = route_slot.shape[0]
    slots = w_gate.shape[0] * lax.axis_size("tok")

    hidden_state = resid.astype(jnp.float32) + jnp.dot(
        attn_out, w_o, preferred_element_type=jnp.float32
    )
    normed = rms_scale(hidden_state, norm1_gain).astype(jnp.bfloat16)
    expert_pick = slot_expert[None, :] == jnp.arange(router_w.shape[1], dtype=jnp.int32)[:, None]
    logits = jnp.dot(normed.astype(jnp.float32), router_w, precision=lax.Precision.HIGHEST)
    slot_logits = jnp.sum(jnp.where(expert_pick[None], logits[:, :, None], 0.0), axis=1)
    hits = jnp.any(
        route_slot[:, :, None] == jnp.arange(slots, dtype=jnp.int32)[None, None, :], axis=1
    )
    top_logit = jnp.max(jnp.where(hits, slot_logits, -jnp.inf), axis=1, keepdims=True)
    powers = jnp.where(hits, jnp.exp(jnp.where(hits, slot_logits, top_logit) - top_logit), 0.0)
    probs = powers / jnp.sum(powers, axis=1, keepdims=True)
    probs = jnp.where((keep > 0)[:, None], probs, 0.0)
    high = lax.reduce_precision(probs, 8, 7)
    low = probs - high
    sent = jnp.concatenate(
        [normed, high.astype(jnp.bfloat16), low.astype(jnp.bfloat16)], axis=1
    )
    moe = expert_sum(sent, w_gate, w_up, w_down)
    mixed = hidden_state + moe
    return rms_scale(mixed, norm2_gain).astype(jnp.bfloat16)


def solution(mesh):
    placed = (
        P(("tok", "blk"), None),
        P(("tok", "blk"), None),
        P(),
        P(),
        P(),
        P(("tok", "blk"), None),
        P(),
        P(("tok", "blk")),
        P("tok", "blk", None),
        P("tok", "blk", None),
        P("tok", "blk", None),
        P(),
    )
    groups, blocks = mesh.shape["tok"], mesh.shape["blk"]

    def layer(*args):
        slot_dev = args[8].shape[0] // groups
        cube = groups == 8 and blocks == 4 and slot_dev % blocks == 0
        plan = whole_slot_plan if cube else body
        return jax.shard_map(
            plan,
            mesh=mesh,
            in_specs=placed,
            out_specs=P(("tok", "blk"), None),
            check_vma=False,
        )(*args)

    return layer
```

```python
import jax
import jax.numpy as jnp
from jax import lax
from jax.experimental import pallas as pl
from jax.experimental.pallas import tpu as pltpu
from jax.sharding import PartitionSpec as P

eps = 1e-05


def rms_scale(values, gain):
    mean_sq = jnp.mean(values * values, axis=-1, keepdims=True)
    return values * lax.rsqrt(mean_sq + eps) * gain


def body(
    attn_out,
    resid,
    w_o,
    norm1_gain,
    router_w,
    route_slot,
    slot_expert,
    keep,
    w_gate,
    w_up,
    w_down,
    norm2_gain,
):
    rows, top = route_slot.shape
    width = resid.shape[1]
    slot_dev = w_gate.shape[0]
    groups = lax.axis_size("tok")
    slots = slot_dev * groups
    cap = max(2, 2 * rows * top // slots)
    hidden_state = resid.astype(jnp.float32) + jnp.dot(
        attn_out, w_o, preferred_element_type=jnp.float32
    )
    normed = rms_scale(hidden_state, norm1_gain).astype(jnp.bfloat16)
    logits = jnp.dot(normed.astype(jnp.float32), router_w, precision=lax.Precision.HIGHEST)
    slot_hits = route_slot[:, :, None] == jnp.arange(slots, dtype=jnp.int32)[None, None, :]
    expert_of = jnp.sum(jnp.where(slot_hits, slot_expert[None, None, :], 0), axis=-1)
    expert_hits = (
        expert_of[:, :, None] == jnp.arange(router_w.shape[1], dtype=jnp.int32)[None, None, :]
    )
    chosen = jnp.sum(jnp.where(expert_hits, logits[:, None, :], jnp.float32(0.0)), axis=-1)
    probs = jax.nn.softmax(chosen, axis=-1)
    live_rows = keep > 0
    live = jnp.repeat(live_rows, top)
    flat_hits = (slot_hits.reshape(rows * top, slots) & live[:, None]).astype(jnp.int32)
    before = jnp.cumsum(flat_hits, axis=0) - flat_hits
    position = jnp.sum(before * flat_hits, axis=1)
    flat_slot = route_slot.reshape(-1)
    owner = flat_slot // slot_dev
    local = flat_slot % slot_dev
    target_row = owner * cap + position
    target_local = jnp.where(live, local, slot_dev)
    token_index = jnp.arange(rows * top, dtype=jnp.int32) // top
    outgoing = jnp.zeros((slot_dev, groups * cap, width), jnp.bfloat16)
    outgoing = outgoing.at[target_local, target_row].set(normed[token_index], mode="drop")
    received = lax.all_to_all(outgoing, "tok", split_axis=1, concat_axis=1, tiled=True)
    gate_part = jnp.einsum(
        "snd,sdf->snf",
        received,
        lax.all_gather(w_gate, "blk", axis=1, tiled=True),
        preferred_element_type=jnp.float32,
    )
    up_part = jnp.einsum(
        "snd,sdf->snf",
        received,
        lax.all_gather(w_up, "blk", axis=1, tiled=True),
        preferred_element_type=jnp.float32,
    )
    act = (jax.nn.silu(gate_part) * up_part).astype(jnp.bfloat16)
    expert_y = jnp.einsum(
        "snf,sdf->snd",
        act,
        lax.all_gather(w_down, "blk", axis=1, tiled=True),
        preferred_element_type=jnp.float32,
    ).astype(jnp.bfloat16)
    returned = lax.all_to_all(expert_y, "tok", split_axis=1, concat_axis=1, tiled=True)
    picked = returned[local, target_row]
    scale = probs.reshape(-1) * live.astype(jnp.float32)
    moe = jnp.sum((picked.astype(jnp.float32) * scale[:, None]).reshape(rows, top, width), axis=1)
    mixed = hidden_state + moe
    return rms_scale(mixed, norm2_gain).astype(jnp.bfloat16)


def flip(value, step):
    return value + step * (1 - 2 * ((value // step) % 2))


def turned(value, r):
    value = flip(value, 1) if r & 1 else value
    return flip(value, 2) if r & 2 else value


def expert_kernel(
    attn_ref,
    resid_ref,
    gain1_ref,
    router_ref,
    route_ref,
    expert_ref,
    keep_ref,
    gain2_ref,
    wo_ref,
    wg_ref,
    wu_ref,
    wd_ref,
    out_ref,
    hidden,
    tokens,
    gates,
    ups,
    downs,
    acts,
    sums,
    from_core,
    from_far,
    from_near,
    from_blk,
    send_sem,
    recv_sem,
    own_sem,
):
    a, b = lax.axis_index("tok"), lax.axis_index("blk")
    a_core, a_x, a_y = flip(a, 1), flip(a, 2), flip(a, 4)
    core, mx, my = a % 2, (a // 2) % 2, a // 4
    far = flip(a_x, 4)
    rows = attn_ref.shape[0]
    tile = 4 * rows
    half = rows // 2
    sub = gates.shape[0]
    block = downs.shape[2]
    width, ff = gates.shape[1:]
    number = iter(range(send_sem.shape[0]))
    started = []

    def send(src, dst, device):
        k = next(number)
        copy = pltpu.make_async_remote_copy(
            src_ref=src,
            dst_ref=dst,
            send_sem=send_sem.at[k],
            recv_sem=recv_sem.at[k],
            device_id=device,
            device_id_type=pl.DeviceIdType.MESH,
        )
        copy.start()
        started.append(copy)
        return copy

    barrier = pltpu.get_barrier_semaphore()
    partners = [(a_core, b), (a_x, b), (a_y, b)] + [(a, turned(b, r)) for r in (1, 2, 3)]
    for partner in partners:
        pl.semaphore_signal(
            barrier, inc=1, device_id=partner, device_id_type=pl.DeviceIdType.MESH
        )
    pl.semaphore_wait(barrier, len(partners))

    own = a * 4 + b
    here = pl.ds(pl.multiple_of(b * block, 128), block)
    weights = {}

    def send_slot(s):
        weights[s] = []
        for r in (3, 2, 1):
            to = turned(b, r)
            weights[s].append(send(wg_ref.at[to * sub + s], gates.at[s, here], (a, to)))
            weights[s].append(send(wu_ref.at[to * sub + s], ups.at[s, here], (a, to)))

    projection = []
    for k in range(3):
        part = pl.ds(k * tile, tile)
        projection.append((wo_ref.at[part, pl.ds(0, 2 * tile)], acts.at[k]))
        projection.append(
            (wo_ref.at[part, pl.ds(2 * tile, tile)], acts.at[3 + k, :, pl.ds(0, tile)])
        )
    projection = [
        pltpu.make_async_copy(src, dst, own_sem.at[3 + k])
        for k, (src, dst) in enumerate(projection)
    ]
    for copy in projection:
        copy.start()
    send_slot(0)
    mine = [
        pltpu.make_async_copy(wg_ref.at[pl.ds(b * sub, sub)], gates.at[:, here], own_sem.at[0]),
        pltpu.make_async_copy(wu_ref.at[pl.ds(b * sub, sub)], ups.at[:, here], own_sem.at[1]),
        pltpu.make_async_copy(wd_ref.at[pl.ds(b * sub, sub)], downs.at[b], own_sem.at[2]),
    ]
    for copy in mine:
        copy.start()
    for copy in projection:
        copy.wait()
    for k in range(3):
        x = attn_ref[:, k * tile : (k + 1) * tile]
        left = jnp.dot(x, acts[k], preferred_element_type=jnp.float32)
        right = jnp.dot(x, acts[3 + k, :, :tile], preferred_element_type=jnp.float32)
        if k == 0:
            hidden[:, : 2 * tile] = left
            hidden[:, 2 * tile :] = right
        else:
            hidden[:, : 2 * tile] += left
            hidden[:, 2 * tile :] += right
    hidden[...] += resid_ref[...].astype(jnp.float32)
    normed = rms_scale(hidden[...], gain1_ref[...]).astype(jnp.bfloat16)
    logits = jnp.dot(
        normed.astype(jnp.float32),
        router_ref[...],
        precision=lax.Precision.HIGHEST,
        preferred_element_type=jnp.float32,
    )
    slots = expert_ref.shape[1]
    slot_logits = jnp.zeros((rows, slots), jnp.float32)
    for e in range(router_ref.shape[1]):
        slot_logits = jnp.where(expert_ref[...] == e, logits[:, e : e + 1], slot_logits)
    slot_of = lax.broadcasted_iota(jnp.int32, (rows, slots), 1)
    hits = slot_of == route_ref[:, 0:1]
    for k in range(1, route_ref.shape[1]):
        hits = hits | (slot_of == route_ref[:, k : k + 1])
    top_logit = jnp.max(jnp.where(hits, slot_logits, -jnp.inf), axis=1, keepdims=True)
    powers = jnp.exp(jnp.where(hits, slot_logits, top_logit) - top_logit)
    powers = jnp.where(hits, powers, 0.0)
    probs = powers / jnp.sum(powers, axis=1, keepdims=True)
    probs = jnp.where(keep_ref[...] > 0, probs, 0.0)
    high = probs.astype(jnp.bfloat16)
    low = (probs - high.astype(jnp.float32)).astype(jnp.bfloat16)
    tokens[own, :, :width] = normed
    tokens[own, :, width:] = jnp.concatenate([high, low], axis=1)
    by_blk = {r: send(tokens.at[own], tokens.at[own], (a, turned(b, r))) for r in (2, 1)}

    def block_at(group, r):
        return tokens.at[group * 4 + turned(b, r)]

    def pass_on(group, r, to):
        return send(block_at(group, r), block_at(group, r), (to, b))

    by_x, by_y, by_core = {}, {}, []
    for r in (0, 2, 1, 3):
        if r:
            by_blk[r].wait_recv()
        if r == 2:
            by_blk[3] = send(block_at(a, 2), block_at(a, 2), (a, turned(b, 1)))
        by_x[r] = pass_on(a, r, a_x)
        by_y[r] = pass_on(a, r, a_y)
        by_core.append(pass_on(a, r, a_core))
    far_y, far_x = {}, {}
    for r in (0, 2, 1, 3):
        by_x[r].wait_recv()
        piece = tokens.at[a_x * 4 + turned(b, r), pl.ds(0, half)]
        far_y[r] = send(piece, piece, (a_y, b))
        by_core.append(pass_on(a_x, r, a_core))
        by_y[r].wait_recv()
        piece = tokens.at[a_y * 4 + turned(b, r), pl.ds(half, half)]
        far_x[r] = send(piece, piece, (a_x, b))
        by_core.append(pass_on(a_y, r, a_core))
    for s in range(1, sub):
        send_slot(s)
    for r in (0, 2, 1, 3):
        far_y[r].wait_recv()
        far_x[r].wait_recv()
        by_core.append(pass_on(far, r, a_core))
    for copy in by_core:
        copy.wait_recv()

    for copy in mine:
        copy.wait()
    later = {}

    def send_down(r):
        to = turned(b, r)
        later[r] = send(wd_ref.at[pl.ds(to * sub, sub)], downs.at[b], (a, to))

    first = sub * own
    lanes = tokens.shape[2] - width
    lane = lax.broadcasted_iota(jnp.int32, (tile, lanes), 1)

    for s in range(sub):

        def expert_rows(t, carry):
            x = tokens[pl.ds(t * 4, 4)].reshape(tile, tokens.shape[2])
            parts = x[:, width:].astype(jnp.float32)
            x = x[:, :width]
            at = (lane == first + s) | (lane == first + s + lanes // 2)
            scale = jnp.sum(jnp.where(at, parts, 0.0), axis=1, keepdims=True)
            gate = jnp.dot(x, gates[s], preferred_element_type=jnp.float32)
            up = jnp.dot(x, ups[s], preferred_element_type=jnp.float32)
            act = gate / (1.0 + jnp.exp(-gate)) * up * scale
            acts[t, :, s * ff : (s + 1) * ff] = act.astype(jnp.bfloat16)
            return carry

        for copy in weights[s]:
            copy.wait_recv()
        if s == sub - 1:
            send_down(1)
            send_down(3)
        lax.fori_loop(0, 8, expert_rows, 0)
    send_down(2)

    def weighted(r):
        column = turned(b, r)

        def down_rows(t, carry):
            y = jnp.zeros((tile, block), jnp.float32)
            for s in range(sub):
                y = y + lax.dot_general(
                    acts[t, :, s * ff : (s + 1) * ff],
                    downs[column, s],
                    (((1,), (1,)), ((), ())),
                    preferred_element_type=jnp.float32,
                )
            sums[r, t % 2, t // 4, (t // 2) % 2] = y.astype(jnp.bfloat16)
            return carry

        if r:
            later[r].wait_recv()
        lax.fori_loop(0, 8, down_rows, 0)

    def add(r, i, j, got):
        sums[r, core, i, j] = (
            sums[r, core, i, j].astype(jnp.float32) + got.astype(jnp.float32)
        ).astype(jnp.bfloat16)

    step = [{}, {}, {}, {}]

    def send_core(r):
        step[0][r] = send(sums.at[r, 1 - core], from_core.at[r], (a_core, b))

    def send_far(r):
        step[0][r].wait_recv()
        for i in range(2):
            for j in range(2):
                add(r, i, j, from_core[r, i, j])
        if r % 2 == 0:
            step[1][r] = send(sums.at[r, core, :, 1 - mx], from_far.at[r], (a_x, b))
        else:
            step[1][r] = send(sums.at[r, core, 1 - my], from_far.at[r], (a_y, b))

    def send_near(r):
        step[1][r].wait_recv()
        for i in range(2):
            if r % 2 == 0:
                add(r, i, mx, from_far[r, i])
            else:
                add(r, my, i, from_far[r, i])
        if r % 2 == 0:
            step[2][r] = send(sums.at[r, core, 1 - my, mx], from_near.at[r], (a_y, b))
        else:
            step[2][r] = send(sums.at[r, core, my, 1 - mx], from_near.at[r], (a_x, b))

    def send_blk(r):
        step[2][r].wait_recv()
        add(r, my, mx, from_near[r])
        columns = pl.ds(pl.multiple_of(turned(b, r) * block, 128), block)
        for q in (3, 2, 1):
            to = turned(b, q)
            piece = pl.ds(pl.multiple_of(to * rows, 16), rows)
            step[3][r, q] = send(
                sums.at[r, core, my, mx, piece], from_blk.at[q - 1, :, columns], (a, to)
            )
        kept = sums[r, core, my, mx, pl.ds(pl.multiple_of(b * rows, 16), rows)]
        hidden[:, columns] += kept.astype(jnp.float32)

    for r, n in ((0, 0), (1, 1), (3, 2), (2, 3)):
        weighted(r)
        send_core(r)
        if n >= 1:
            send_far((0, 1, 3)[n - 1])
    send_near(0)
    send_far(2)
    send_near(1)
    send_blk(0)
    send_near(3)
    send_blk(1)
    send_near(2)
    send_blk(3)
    send_blk(2)
    for copy in step[3].values():
        copy.wait_recv()
    mixed = hidden[...] + (
        from_blk[0].astype(jnp.float32)
        + from_blk[1].astype(jnp.float32)
        + from_blk[2].astype(jnp.float32)
    )
    out_ref[...] = rms_scale(mixed, gain2_ref[...]).astype(jnp.bfloat16)
    for copy in started:
        copy.wait_send()


def whole_slot_plan(
    attn_out,
    resid,
    w_o,
    norm1_gain,
    router_w,
    route_slot,
    slot_expert,
    keep,
    w_gate,
    w_up,
    w_down,
    norm2_gain,
):
    rows, width = resid.shape
    slot_dev, block, ff = w_gate.shape
    sub = slot_dev // 4
    slots = slot_expert.shape[0]
    tile = 4 * rows
    copies = 3 + 6 * sub + 12 + 16 + 4 + 3 + 12 + 12
    bf16 = jnp.bfloat16
    macs = 32 * rows * sub * ff * width * 3
    return pl.pallas_call(
        expert_kernel,
        out_shape=jax.ShapeDtypeStruct((rows, width), bf16),
        in_specs=[pl.BlockSpec(memory_space=pltpu.VMEM)] * 8
        + [pl.BlockSpec(memory_space=pl.ANY)] * 4,
        out_specs=pl.BlockSpec(memory_space=pltpu.VMEM),
        scratch_shapes=[
            pltpu.VMEM((rows, width), jnp.float32),
            pltpu.VMEM((32, rows, width + 2 * slots), bf16),
            pltpu.VMEM((sub, width, ff), bf16),
            pltpu.VMEM((sub, width, ff), bf16),
            pltpu.VMEM((4, sub, block, ff), bf16),
            pltpu.VMEM((8, tile, sub * ff), bf16),
            pltpu.VMEM((4, 2, 2, 2, tile, block), bf16),
            pltpu.VMEM((4, 2, 2, tile, block), bf16),
            pltpu.VMEM((4, 2, tile, block), bf16),
            pltpu.VMEM((4, tile, block), bf16),
            pltpu.VMEM((3, rows, width), bf16),
            pltpu.SemaphoreType.DMA((copies,)),
            pltpu.SemaphoreType.DMA((copies,)),
            pltpu.SemaphoreType.DMA((9,)),
        ],
        compiler_params=pltpu.CompilerParams(
            collective_id=0, has_side_effects=True, vmem_limit_bytes=63 * 1024 * 1024
        ),
        cost_estimate=pl.CostEstimate(
            flops=2 * macs, bytes_accessed=3 * slot_dev * block * ff * 2, transcendentals=0
        ),
    )(
        attn_out,
        resid,
        norm1_gain.reshape(1, width),
        router_w,
        route_slot,
        slot_expert.reshape(1, slots),
        keep.reshape(rows, 1),
        norm2_gain.reshape(1, width),
        w_o,
        w_gate,
        w_up,
        w_down,
    )


def solution(mesh):
    placed = (
        P(("tok", "blk"), None),
        P(("tok", "blk"), None),
        P(),
        P(),
        P(),
        P(("tok", "blk"), None),
        P(),
        P(("tok", "blk")),
        P("tok", "blk", None),
        P("tok", "blk", None),
        P("tok", "blk", None),
        P(),
    )
    groups, blocks = mesh.shape["tok"], mesh.shape["blk"]

    def layer(*args):
        slot_dev = args[8].shape[0] // groups
        rows, width = args[1].shape[0] // (groups * blocks), args[1].shape[1]
        fits = slot_dev == 8 and args[8].shape[2] == 4 * rows and width == 12 * rows
        cube = groups == 8 and blocks == 4 and fits and args[2].shape == (width, width)
        plan = whole_slot_plan if cube else body
        return jax.shard_map(
            plan,
            mesh=mesh,
            in_specs=placed,
            out_specs=P(("tok", "blk"), None),
            check_vma=False,
        )(*args)

    return layer
```

```python
import jax
import jax.numpy as jnp
from jax import lax
from jax.experimental import pallas as pl
from jax.experimental.pallas import tpu as pltpu
from jax.sharding import PartitionSpec as P

eps = 1e-05


def rms_scale(values, gain):
    mean_sq = jnp.mean(values * values, axis=-1, keepdims=True)
    return values * lax.rsqrt(mean_sq + eps) * gain


def body(
    attn_out,
    resid,
    w_o,
    norm1_gain,
    router_w,
    route_slot,
    slot_expert,
    keep,
    w_gate,
    w_up,
    w_down,
    norm2_gain,
):
    rows, top = route_slot.shape
    width = resid.shape[1]
    slot_dev = w_gate.shape[0]
    groups = lax.axis_size("tok")
    slots = slot_dev * groups
    cap = max(2, 2 * rows * top // slots)
    hidden_state = resid.astype(jnp.float32) + jnp.dot(
        attn_out, w_o, preferred_element_type=jnp.float32
    )
    normed = rms_scale(hidden_state, norm1_gain).astype(jnp.bfloat16)
    logits = jnp.dot(normed.astype(jnp.float32), router_w, precision=lax.Precision.HIGHEST)
    slot_hits = route_slot[:, :, None] == jnp.arange(slots, dtype=jnp.int32)[None, None, :]
    expert_of = jnp.sum(jnp.where(slot_hits, slot_expert[None, None, :], 0), axis=-1)
    expert_hits = (
        expert_of[:, :, None] == jnp.arange(router_w.shape[1], dtype=jnp.int32)[None, None, :]
    )
    chosen = jnp.sum(jnp.where(expert_hits, logits[:, None, :], jnp.float32(0.0)), axis=-1)
    probs = jax.nn.softmax(chosen, axis=-1)
    live_rows = keep > 0
    live = jnp.repeat(live_rows, top)
    flat_hits = (slot_hits.reshape(rows * top, slots) & live[:, None]).astype(jnp.int32)
    before = jnp.cumsum(flat_hits, axis=0) - flat_hits
    position = jnp.sum(before * flat_hits, axis=1)
    flat_slot = route_slot.reshape(-1)
    owner = flat_slot // slot_dev
    local = flat_slot % slot_dev
    target_row = owner * cap + position
    target_local = jnp.where(live, local, slot_dev)
    token_index = jnp.arange(rows * top, dtype=jnp.int32) // top
    outgoing = jnp.zeros((slot_dev, groups * cap, width), jnp.bfloat16)
    outgoing = outgoing.at[target_local, target_row].set(normed[token_index], mode="drop")
    received = lax.all_to_all(outgoing, "tok", split_axis=1, concat_axis=1, tiled=True)
    gate_part = jnp.einsum(
        "snd,sdf->snf",
        received,
        lax.all_gather(w_gate, "blk", axis=1, tiled=True),
        preferred_element_type=jnp.float32,
    )
    up_part = jnp.einsum(
        "snd,sdf->snf",
        received,
        lax.all_gather(w_up, "blk", axis=1, tiled=True),
        preferred_element_type=jnp.float32,
    )
    act = (jax.nn.silu(gate_part) * up_part).astype(jnp.bfloat16)
    expert_y = jnp.einsum(
        "snf,sdf->snd",
        act,
        lax.all_gather(w_down, "blk", axis=1, tiled=True),
        preferred_element_type=jnp.float32,
    ).astype(jnp.bfloat16)
    returned = lax.all_to_all(expert_y, "tok", split_axis=1, concat_axis=1, tiled=True)
    picked = returned[local, target_row]
    scale = probs.reshape(-1) * live.astype(jnp.float32)
    moe = jnp.sum((picked.astype(jnp.float32) * scale[:, None]).reshape(rows, top, width), axis=1)
    mixed = hidden_state + moe
    return rms_scale(mixed, norm2_gain).astype(jnp.bfloat16)


def flip(value, step):
    return value + step * (1 - 2 * ((value // step) % 2))


def turned(value, r):
    value = flip(value, 1) if r & 1 else value
    return flip(value, 2) if r & 2 else value


def expert_kernel(
    attn_ref,
    resid_ref,
    gain1_ref,
    gain2_ref,
    router_ref,
    route_ref,
    expert_ref,
    keep_ref,
    wo_ref,
    wg_ref,
    wu_ref,
    wd_ref,
    out_ref,
    hidden,
    tokens,
    gates,
    ups,
    downs,
    acts,
    sums,
    from_core,
    from_far,
    from_near,
    from_blk,
    send_sem,
    recv_sem,
    own_sem,
):
    a, b = lax.axis_index("tok"), lax.axis_index("blk")
    a_core, a_x, a_y = flip(a, 1), flip(a, 2), flip(a, 4)
    core, mx, my = a % 2, (a // 2) % 2, a // 4
    far = flip(a_x, 4)
    rows = attn_ref.shape[0]
    tile = 4 * rows
    half = rows // 2
    sub = gates.shape[0]
    block = downs.shape[2]
    width, ff = gates.shape[1:]
    number = iter(range(send_sem.shape[0]))
    started = []

    def send(src, dst, device):
        k = next(number)
        copy = pltpu.make_async_remote_copy(
            src_ref=src,
            dst_ref=dst,
            send_sem=send_sem.at[k],
            recv_sem=recv_sem.at[k],
            device_id=device,
            device_id_type=pl.DeviceIdType.MESH,
        )
        copy.start()
        started.append(copy)
        return copy

    barrier = pltpu.get_barrier_semaphore()
    partners = [(a_core, b), (a_x, b), (a_y, b)] + [(a, turned(b, r)) for r in (1, 2, 3)]
    for partner in partners:
        pl.semaphore_signal(
            barrier, inc=1, device_id=partner, device_id_type=pl.DeviceIdType.MESH
        )
    pl.semaphore_wait(barrier, len(partners))

    own = a * 4 + b
    here = pl.ds(pl.multiple_of(b * block, 128), block)
    weights = {s: [] for s in range(sub)}
    waiting = [
        (s, r, src, dst)
        for s in range(sub)
        for r in (3, 2, 1)
        for src, dst in ((wg_ref, gates), (wu_ref, ups))
    ]

    def send_weight():
        if waiting:
            s, r, src, dst = waiting.pop(0)
            to = turned(b, r)
            weights[s].append(send(src.at[to * sub + s], dst.at[s, here], (a, to)))

    projection = []
    for k in range(3):
        part = pl.ds(k * tile, tile)
        projection.append((wo_ref.at[part, pl.ds(0, 2 * tile)], acts.at[k]))
        projection.append(
            (wo_ref.at[part, pl.ds(2 * tile, tile)], acts.at[3 + k, :, pl.ds(0, tile)])
        )
    projection = [
        pltpu.make_async_copy(src, dst, own_sem.at[3 + k])
        for k, (src, dst) in enumerate(projection)
    ]
    for copy in projection:
        copy.start()
    send_weight()
    mine = [
        pltpu.make_async_copy(wg_ref.at[pl.ds(b * sub, sub)], gates.at[:, here], own_sem.at[0]),
        pltpu.make_async_copy(wu_ref.at[pl.ds(b * sub, sub)], ups.at[:, here], own_sem.at[1]),
        pltpu.make_async_copy(wd_ref.at[pl.ds(b * sub, sub)], downs.at[b], own_sem.at[2]),
    ]
    for copy in mine:
        copy.start()
    for copy in projection:
        copy.wait()
    for k in range(3):
        x = attn_ref[:, k * tile : (k + 1) * tile]
        left = jnp.dot(x, acts[k], preferred_element_type=jnp.float32)
        right = jnp.dot(x, acts[3 + k, :, :tile], preferred_element_type=jnp.float32)
        if k == 0:
            hidden[:, : 2 * tile] = left
            hidden[:, 2 * tile :] = right
        else:
            hidden[:, : 2 * tile] += left
            hidden[:, 2 * tile :] += right
    hidden[...] += resid_ref[...].astype(jnp.float32)
    normed = rms_scale(hidden[...], gain1_ref[...].reshape(1, width)).astype(jnp.bfloat16)
    logits = lax.dot_general(
        normed.astype(jnp.float32),
        router_ref[...],
        (((1,), (1,)), ((), ())),
        precision=lax.Precision.HIGHEST,
        preferred_element_type=jnp.float32,
    )
    slots = expert_ref.shape[1]
    slot_logits = jnp.zeros((rows, slots), jnp.float32)
    for e in range(router_ref.shape[0]):
        slot_logits = jnp.where(expert_ref[...] == e, logits[:, e : e + 1], slot_logits)
    slot_of = lax.broadcasted_iota(jnp.int32, (rows, slots), 1)
    route = jnp.where(keep_ref[...] > 0, route_ref[...], -1).T
    hits = slot_of == route[:, 0:1]
    for k in range(1, route.shape[1]):
        hits = hits | (slot_of == route[:, k : k + 1])
    top_logit = jnp.max(jnp.where(hits, slot_logits, -jnp.inf), axis=1, keepdims=True)
    powers = jnp.exp(jnp.where(hits, slot_logits, top_logit) - top_logit)
    powers = jnp.where(hits, powers, 0.0)
    probs = jnp.where(hits, powers / jnp.sum(powers, axis=1, keepdims=True), 0.0)
    high = probs.astype(jnp.bfloat16)
    low = (probs - high.astype(jnp.float32)).astype(jnp.bfloat16)
    tokens[own, :, :width] = normed
    tokens[own, :, width:] = jnp.concatenate([high, low], axis=1)
    by_blk = {r: send(tokens.at[own], tokens.at[own], (a, turned(b, r))) for r in (2, 1)}

    def block_at(group, r):
        return tokens.at[group * 4 + turned(b, r)]

    def pass_on(group, r, to):
        return send(block_at(group, r), block_at(group, r), (to, b))

    by_x, by_y, by_core = {}, {}, []
    for r in (0, 2, 1, 3):
        if r:
            by_blk[r].wait_recv()
        if r == 2:
            by_blk[3] = send(block_at(a, 2), block_at(a, 2), (a, turned(b, 1)))
        by_x[r] = pass_on(a, r, a_x)
        by_y[r] = pass_on(a, r, a_y)
        by_core.append(pass_on(a, r, a_core))
        send_weight()
    far_y, far_x = {}, {}
    for r in (0, 2, 1, 3):
        by_x[r].wait_recv()
        piece = tokens.at[a_x * 4 + turned(b, r), pl.ds(0, half)]
        far_y[r] = send(piece, piece, (a_y, b))
        by_core.append(pass_on(a_x, r, a_core))
        by_y[r].wait_recv()
        piece = tokens.at[a_y * 4 + turned(b, r), pl.ds(half, half)]
        far_x[r] = send(piece, piece, (a_x, b))
        by_core.append(pass_on(a_y, r, a_core))
        send_weight()
    for r in (0, 2, 1, 3):
        far_y[r].wait_recv()
        far_x[r].wait_recv()
        by_core.append(pass_on(far, r, a_core))
        send_weight()
    while waiting:
        send_weight()
    for copy in by_core:
        copy.wait_recv()

    for copy in mine:
        copy.wait()
    later = {}

    def send_down(r):
        to = turned(b, r)
        later[r] = send(wd_ref.at[pl.ds(to * sub, sub)], downs.at[b], (a, to))

    first = sub * own
    lanes = tokens.shape[2] - width
    lane = lax.broadcasted_iota(jnp.int32, (tile, lanes), 1)

    for s in range(sub):

        def expert_rows(t, carry):
            x = tokens[pl.ds(t * 4, 4)].reshape(tile, tokens.shape[2])
            parts = x[:, width:].astype(jnp.float32)
            x = x[:, :width]
            at = (lane == first + s) | (lane == first + s + lanes // 2)
            scale = jnp.sum(jnp.where(at, parts, 0.0), axis=1, keepdims=True)
            gate = jnp.dot(x, gates[s], preferred_element_type=jnp.float32)
            up = jnp.dot(x, ups[s], preferred_element_type=jnp.float32)
            act = gate / (1.0 + jnp.exp(-gate)) * up * scale
            acts[t, :, s * ff : (s + 1) * ff] = act.astype(jnp.bfloat16)
            return carry

        for copy in weights[s]:
            copy.wait_recv()
        if s == 0:
            for r in (1, 3, 2):
                send_down(r)
        lax.fori_loop(0, 8, expert_rows, 0)

    def weighted(r):
        column = turned(b, r)

        def down_rows(t, carry):
            y = jnp.zeros((tile, block), jnp.float32)
            for s in range(sub):
                y = y + lax.dot_general(
                    acts[t, :, s * ff : (s + 1) * ff],
                    downs[column, s],
                    (((1,), (1,)), ((), ())),
                    preferred_element_type=jnp.float32,
                )
            sums[r, t % 2, t // 4, (t // 2) % 2] = y.astype(jnp.bfloat16)
            return carry

        if r:
            later[r].wait_recv()
        lax.fori_loop(0, 8, down_rows, 0)

    def add(r, i, j, got):
        sums[r, core, i, j] = (
            sums[r, core, i, j].astype(jnp.float32) + got.astype(jnp.float32)
        ).astype(jnp.bfloat16)

    step = [{}, {}, {}, {}]

    def send_core(r):
        step[0][r] = send(sums.at[r, 1 - core], from_core.at[r], (a_core, b))

    def send_far(r):
        step[0][r].wait_recv()
        for i in range(2):
            for j in range(2):
                add(r, i, j, from_core[r, i, j])
        if r % 2 == 0:
            step[1][r] = send(sums.at[r, core, :, 1 - mx], from_far.at[r], (a_x, b))
        else:
            step[1][r] = send(sums.at[r, core, 1 - my], from_far.at[r], (a_y, b))

    def send_near(r):
        step[1][r].wait_recv()
        for i in range(2):
            if r % 2 == 0:
                add(r, i, mx, from_far[r, i])
            else:
                add(r, my, i, from_far[r, i])
        if r % 2 == 0:
            step[2][r] = send(sums.at[r, core, 1 - my, mx], from_near.at[r], (a_y, b))
        else:
            step[2][r] = send(sums.at[r, core, my, 1 - mx], from_near.at[r], (a_x, b))

    def send_blk(r):
        step[2][r].wait_recv()
        add(r, my, mx, from_near[r])
        columns = pl.ds(pl.multiple_of(turned(b, r) * block, 128), block)
        for q in (3, 2, 1):
            to = turned(b, q)
            piece = pl.ds(pl.multiple_of(to * rows, 16), rows)
            step[3][r, q] = send(
                sums.at[r, core, my, mx, piece], from_blk.at[q - 1, :, columns], (a, to)
            )
        kept = sums[r, core, my, mx, pl.ds(pl.multiple_of(b * rows, 16), rows)]
        hidden[:, columns] += kept.astype(jnp.float32)

    for r, n in ((0, 0), (1, 1), (3, 2), (2, 3)):
        weighted(r)
        send_core(r)
        if n >= 1:
            send_far((0, 1, 3)[n - 1])
    send_near(0)
    send_far(2)
    send_near(1)
    send_blk(0)
    send_near(3)
    send_blk(1)
    send_near(2)
    send_blk(3)
    send_blk(2)
    for copy in step[3].values():
        copy.wait_recv()
    mixed = hidden[...] + (
        from_blk[0].astype(jnp.float32)
        + from_blk[1].astype(jnp.float32)
        + from_blk[2].astype(jnp.float32)
    )
    out_ref[...] = rms_scale(mixed, gain2_ref[...].reshape(1, width)).astype(jnp.bfloat16)
    for copy in started:
        copy.wait_send()


def whole_slot_plan(
    attn_out,
    resid,
    w_o,
    norm1_gain,
    router_w,
    route_slot,
    slot_expert,
    keep,
    w_gate,
    w_up,
    w_down,
    norm2_gain,
):
    rows, width = resid.shape
    slot_dev, block, ff = w_gate.shape
    sub = slot_dev // 4
    slots = slot_expert.shape[0]
    tile = 4 * rows
    copies = 3 + 6 * sub + 12 + 16 + 4 + 3 + 12 + 12
    bf16 = jnp.bfloat16
    macs = 32 * rows * sub * ff * width * 3
    return pl.pallas_call(
        expert_kernel,
        out_shape=jax.ShapeDtypeStruct((rows, width), bf16),
        in_specs=[pl.BlockSpec(memory_space=pltpu.VMEM)] * 8
        + [pl.BlockSpec(memory_space=pl.ANY)] * 4,
        out_specs=pl.BlockSpec(memory_space=pltpu.VMEM),
        scratch_shapes=[
            pltpu.VMEM((rows, width), jnp.float32),
            pltpu.VMEM((32, rows, width + 2 * slots), bf16),
            pltpu.VMEM((sub, width, ff), bf16),
            pltpu.VMEM((sub, width, ff), bf16),
            pltpu.VMEM((4, sub, block, ff), bf16),
            pltpu.VMEM((8, tile, sub * ff), bf16),
            pltpu.VMEM((4, 2, 2, 2, tile, block), bf16),
            pltpu.VMEM((4, 2, 2, tile, block), bf16),
            pltpu.VMEM((4, 2, tile, block), bf16),
            pltpu.VMEM((4, tile, block), bf16),
            pltpu.VMEM((3, rows, width), bf16),
            pltpu.SemaphoreType.DMA((copies,)),
            pltpu.SemaphoreType.DMA((copies,)),
            pltpu.SemaphoreType.DMA((9,)),
        ],
        compiler_params=pltpu.CompilerParams(
            collective_id=0, has_side_effects=True, vmem_limit_bytes=63 * 1024 * 1024
        ),
        cost_estimate=pl.CostEstimate(
            flops=2 * macs, bytes_accessed=3 * slot_dev * block * ff * 2, transcendentals=0
        ),
    )(
        attn_out,
        resid,
        norm1_gain,
        norm2_gain,
        router_w.T,
        route_slot.T,
        slot_expert.reshape(1, slots),
        keep.reshape(1, rows),
        w_o,
        w_gate,
        w_up,
        w_down,
    )


def solution(mesh):
    placed = (
        P(("tok", "blk"), None),
        P(("tok", "blk"), None),
        P(),
        P(),
        P(),
        P(("tok", "blk"), None),
        P(),
        P(("tok", "blk")),
        P("tok", "blk", None),
        P("tok", "blk", None),
        P("tok", "blk", None),
        P(),
    )
    groups, blocks = mesh.shape["tok"], mesh.shape["blk"]

    def layer(*args):
        slot_dev = args[8].shape[0] // groups
        rows, width = args[1].shape[0] // (groups * blocks), args[1].shape[1]
        fits = slot_dev == 8 and args[8].shape[2] == 4 * rows and width == 12 * rows
        cube = groups == 8 and blocks == 4 and fits and args[2].shape == (width, width)
        plan = whole_slot_plan if cube else body
        return jax.shard_map(
            plan,
            mesh=mesh,
            in_specs=placed,
            out_specs=P(("tok", "blk"), None),
            check_vma=False,
        )(*args)

    return layer
```

```python
import jax
import jax.numpy as jnp
from jax import lax
from jax.experimental import pallas as pl
from jax.experimental.pallas import tpu as pltpu
from jax.sharding import PartitionSpec as P

eps = 1e-05


def rms_scale(values, gain):
    mean_sq = jnp.mean(values * values, axis=-1, keepdims=True)
    return values * lax.rsqrt(mean_sq + eps) * gain


def body(
    attn_out,
    resid,
    w_o,
    norm1_gain,
    router_w,
    route_slot,
    slot_expert,
    keep,
    w_gate,
    w_up,
    w_down,
    norm2_gain,
):
    rows, top = route_slot.shape
    width = resid.shape[1]
    slot_dev = w_gate.shape[0]
    groups = lax.axis_size("tok")
    slots = slot_dev * groups
    cap = max(2, 2 * rows * top // slots)
    hidden_state = resid.astype(jnp.float32) + jnp.dot(
        attn_out, w_o, preferred_element_type=jnp.float32
    )
    normed = rms_scale(hidden_state, norm1_gain).astype(jnp.bfloat16)
    logits = jnp.dot(normed.astype(jnp.float32), router_w, precision=lax.Precision.HIGHEST)
    slot_hits = route_slot[:, :, None] == jnp.arange(slots, dtype=jnp.int32)[None, None, :]
    expert_of = jnp.sum(jnp.where(slot_hits, slot_expert[None, None, :], 0), axis=-1)
    expert_hits = (
        expert_of[:, :, None] == jnp.arange(router_w.shape[1], dtype=jnp.int32)[None, None, :]
    )
    chosen = jnp.sum(jnp.where(expert_hits, logits[:, None, :], jnp.float32(0.0)), axis=-1)
    probs = jax.nn.softmax(chosen, axis=-1)
    live_rows = keep > 0
    live = jnp.repeat(live_rows, top)
    flat_hits = (slot_hits.reshape(rows * top, slots) & live[:, None]).astype(jnp.int32)
    before = jnp.cumsum(flat_hits, axis=0) - flat_hits
    position = jnp.sum(before * flat_hits, axis=1)
    flat_slot = route_slot.reshape(-1)
    owner = flat_slot // slot_dev
    local = flat_slot % slot_dev
    target_row = owner * cap + position
    target_local = jnp.where(live, local, slot_dev)
    token_index = jnp.arange(rows * top, dtype=jnp.int32) // top
    outgoing = jnp.zeros((slot_dev, groups * cap, width), jnp.bfloat16)
    outgoing = outgoing.at[target_local, target_row].set(normed[token_index], mode="drop")
    received = lax.all_to_all(outgoing, "tok", split_axis=1, concat_axis=1, tiled=True)
    gate_part = jnp.einsum(
        "snd,sdf->snf",
        received,
        lax.all_gather(w_gate, "blk", axis=1, tiled=True),
        preferred_element_type=jnp.float32,
    )
    up_part = jnp.einsum(
        "snd,sdf->snf",
        received,
        lax.all_gather(w_up, "blk", axis=1, tiled=True),
        preferred_element_type=jnp.float32,
    )
    act = (jax.nn.silu(gate_part) * up_part).astype(jnp.bfloat16)
    expert_y = jnp.einsum(
        "snf,sdf->snd",
        act,
        lax.all_gather(w_down, "blk", axis=1, tiled=True),
        preferred_element_type=jnp.float32,
    ).astype(jnp.bfloat16)
    returned = lax.all_to_all(expert_y, "tok", split_axis=1, concat_axis=1, tiled=True)
    picked = returned[local, target_row]
    scale = probs.reshape(-1) * live.astype(jnp.float32)
    moe = jnp.sum((picked.astype(jnp.float32) * scale[:, None]).reshape(rows, top, width), axis=1)
    mixed = hidden_state + moe
    return rms_scale(mixed, norm2_gain).astype(jnp.bfloat16)


def flip(value, step):
    return value + step * (1 - 2 * ((value // step) % 2))


def turned(value, r):
    value = flip(value, 1) if r & 1 else value
    return flip(value, 2) if r & 2 else value


def expert_kernel(
    attn_ref,
    resid_ref,
    gain1_ref,
    gain2_ref,
    router_ref,
    route_ref,
    expert_ref,
    keep_ref,
    wo_ref,
    wg_ref,
    wu_ref,
    wd_ref,
    out_ref,
    hidden,
    tokens,
    gates,
    ups,
    downs,
    acts,
    sums,
    from_core,
    from_far,
    from_near,
    from_blk,
    send_sem,
    recv_sem,
    own_sem,
):
    a, b = lax.axis_index("tok"), lax.axis_index("blk")
    a_core, a_x, a_y = flip(a, 1), flip(a, 2), flip(a, 4)
    core, mx, my = a % 2, (a // 2) % 2, a // 4
    far = flip(a_x, 4)
    rows = attn_ref.shape[0]
    tile = 4 * rows
    half = rows // 2
    sub = gates.shape[0]
    block = downs.shape[2]
    width, ff = gates.shape[1:]
    number = iter(range(send_sem.shape[0]))
    started = []

    def send(src, dst, device):
        k = next(number)
        copy = pltpu.make_async_remote_copy(
            src_ref=src,
            dst_ref=dst,
            send_sem=send_sem.at[k],
            recv_sem=recv_sem.at[k],
            device_id=device,
            device_id_type=pl.DeviceIdType.MESH,
        )
        copy.start()
        started.append(copy)
        return copy

    barrier = pltpu.get_barrier_semaphore()
    partners = [(a_core, b), (a_x, b), (a_y, b)] + [(a, turned(b, r)) for r in (1, 2, 3)]
    for partner in partners:
        pl.semaphore_signal(
            barrier, inc=1, device_id=partner, device_id_type=pl.DeviceIdType.MESH
        )
    pl.semaphore_wait(barrier, len(partners))

    own = a * 4 + b
    here = pl.ds(pl.multiple_of(b * block, 128), block)
    weights = {s: [] for s in range(sub)}
    waiting = [
        (s, r, src, dst)
        for s in range(sub)
        for r in (3, 2, 1)
        for src, dst in ((wg_ref, gates), (wu_ref, ups))
    ]

    def send_weight():
        if waiting:
            s, r, src, dst = waiting.pop(0)
            to = turned(b, r)
            weights[s].append(send(src.at[to * sub + s], dst.at[s, here], (a, to)))

    projection = []
    for k in range(3):
        part = pl.ds(k * tile, tile)
        projection.append((wo_ref.at[part, pl.ds(0, 2 * tile)], acts.at[k]))
        projection.append(
            (wo_ref.at[part, pl.ds(2 * tile, tile)], acts.at[3 + k, :, pl.ds(0, tile)])
        )
    projection = [
        pltpu.make_async_copy(src, dst, own_sem.at[3 + k])
        for k, (src, dst) in enumerate(projection)
    ]
    for copy in projection:
        copy.start()
    send_weight()
    mine = [
        pltpu.make_async_copy(wg_ref.at[pl.ds(b * sub, sub)], gates.at[:, here], own_sem.at[0]),
        pltpu.make_async_copy(wu_ref.at[pl.ds(b * sub, sub)], ups.at[:, here], own_sem.at[1]),
        pltpu.make_async_copy(wd_ref.at[pl.ds(b * sub, sub)], downs.at[b], own_sem.at[2]),
    ]
    for copy in mine:
        copy.start()
    for copy in projection:
        copy.wait()
    for k in range(3):
        x = attn_ref[:, k * tile : (k + 1) * tile]
        left = jnp.dot(x, acts[k], preferred_element_type=jnp.float32)
        right = jnp.dot(x, acts[3 + k, :, :tile], preferred_element_type=jnp.float32)
        if k == 0:
            hidden[:, : 2 * tile] = left
            hidden[:, 2 * tile :] = right
        else:
            hidden[:, : 2 * tile] += left
            hidden[:, 2 * tile :] += right
    hidden[...] += resid_ref[...].astype(jnp.float32)
    normed = rms_scale(hidden[...], gain1_ref[...].reshape(1, width)).astype(jnp.bfloat16)
    logits = lax.dot_general(
        normed.astype(jnp.float32),
        router_ref[...],
        (((1,), (1,)), ((), ())),
        precision=lax.Precision.HIGHEST,
        preferred_element_type=jnp.float32,
    )
    slots = expert_ref.shape[1]
    slot_logits = jnp.zeros((rows, slots), jnp.float32)
    for e in range(router_ref.shape[0]):
        slot_logits = jnp.where(expert_ref[...] == e, logits[:, e : e + 1], slot_logits)
    slot_of = lax.broadcasted_iota(jnp.int32, (rows, slots), 1)
    route = jnp.where(keep_ref[...] > 0, route_ref[...], -1).T
    hits = slot_of == route[:, 0:1]
    for k in range(1, route.shape[1]):
        hits = hits | (slot_of == route[:, k : k + 1])
    top_logit = jnp.max(jnp.where(hits, slot_logits, -jnp.inf), axis=1, keepdims=True)
    powers = jnp.exp(jnp.where(hits, slot_logits, top_logit) - top_logit)
    powers = jnp.where(hits, powers, 0.0)
    probs = jnp.where(hits, powers / jnp.sum(powers, axis=1, keepdims=True), 0.0)
    high = probs.astype(jnp.bfloat16)
    low = (probs - high.astype(jnp.float32)).astype(jnp.bfloat16)
    tokens[own, :, :width] = normed
    tokens[own, :, width:] = jnp.concatenate([high, low], axis=1)
    by_blk = {r: send(tokens.at[own], tokens.at[own], (a, turned(b, r))) for r in (2, 1)}

    def block_at(group, r):
        return tokens.at[group * 4 + turned(b, r)]

    def pass_on(group, r, to):
        return send(block_at(group, r), block_at(group, r), (to, b))

    by_x, by_y, by_core = {}, {}, []
    for r in (0, 2, 1, 3):
        if r:
            by_blk[r].wait_recv()
        if r == 2:
            by_blk[3] = send(block_at(a, 2), block_at(a, 2), (a, turned(b, 1)))
        by_x[r] = pass_on(a, r, a_x)
        by_y[r] = pass_on(a, r, a_y)
        by_core.append(pass_on(a, r, a_core))
        send_weight()
    far_y, far_x = {}, {}
    for r in (0, 2, 1, 3):
        by_x[r].wait_recv()
        piece = tokens.at[a_x * 4 + turned(b, r), pl.ds(0, half)]
        far_y[r] = send(piece, piece, (a_y, b))
        by_core.append(pass_on(a_x, r, a_core))
        by_y[r].wait_recv()
        piece = tokens.at[a_y * 4 + turned(b, r), pl.ds(half, half)]
        far_x[r] = send(piece, piece, (a_x, b))
        by_core.append(pass_on(a_y, r, a_core))
        send_weight()
    for r in (0, 2, 1, 3):
        far_y[r].wait_recv()
        far_x[r].wait_recv()
        by_core.append(pass_on(far, r, a_core))
        send_weight()
    while waiting:
        send_weight()
    for copy in by_core:
        copy.wait_recv()

    for copy in mine:
        copy.wait()
    later = {}

    def send_down(r):
        to = turned(b, r)
        later[r] = send(wd_ref.at[pl.ds(to * sub, sub)], downs.at[b], (a, to))

    first = sub * own
    lanes = tokens.shape[2] - width
    lane = lax.broadcasted_iota(jnp.int32, (tile, lanes), 1)

    for s in range(sub):

        def expert_rows(t, carry):
            x = tokens[pl.ds(t * 4, 4)].reshape(tile, tokens.shape[2])
            parts = x[:, width:].astype(jnp.float32)
            x = x[:, :width]
            at = (lane == first + s) | (lane == first + s + lanes // 2)
            scale = jnp.sum(jnp.where(at, parts, 0.0), axis=1, keepdims=True)
            gate = jnp.dot(x, gates[s], preferred_element_type=jnp.float32)
            up = jnp.dot(x, ups[s], preferred_element_type=jnp.float32)
            act = gate / (1.0 + jnp.exp(-gate)) * up * scale
            acts[t, :, s * ff : (s + 1) * ff] = act.astype(jnp.bfloat16)
            return carry

        for copy in weights[s]:
            copy.wait_recv()
        if s == 0:
            for r in (1, 3, 2):
                send_down(r)
        lax.fori_loop(0, 8, expert_rows, 0, unroll=2)

    def weighted(r):
        column = turned(b, r)

        def down_rows(t, carry):
            y = jnp.zeros((tile, block), jnp.float32)
            for s in range(sub):
                y = y + lax.dot_general(
                    acts[t, :, s * ff : (s + 1) * ff],
                    downs[column, s],
                    (((1,), (1,)), ((), ())),
                    preferred_element_type=jnp.float32,
                )
            sums[r, t % 2, t // 4, (t // 2) % 2] = y.astype(jnp.bfloat16)
            return carry

        if r:
            later[r].wait_recv()
        lax.fori_loop(0, 8, down_rows, 0, unroll=2)

    def add(r, i, j, got):
        sums[r, core, i, j] = (
            sums[r, core, i, j].astype(jnp.float32) + got.astype(jnp.float32)
        ).astype(jnp.bfloat16)

    step = [{}, {}, {}, {}]

    def send_core(r):
        step[0][r] = send(sums.at[r, 1 - core], from_core.at[r], (a_core, b))

    def send_far(r):
        step[0][r].wait_recv()
        for i in range(2):
            for j in range(2):
                add(r, i, j, from_core[r, i, j])
        if r % 2 == 0:
            step[1][r] = send(sums.at[r, core, :, 1 - mx], from_far.at[r], (a_x, b))
        else:
            step[1][r] = send(sums.at[r, core, 1 - my], from_far.at[r], (a_y, b))

    def send_near(r):
        step[1][r].wait_recv()
        for i in range(2):
            if r % 2 == 0:
                add(r, i, mx, from_far[r, i])
            else:
                add(r, my, i, from_far[r, i])
        if r % 2 == 0:
            step[2][r] = send(sums.at[r, core, 1 - my, mx], from_near.at[r], (a_y, b))
        else:
            step[2][r] = send(sums.at[r, core, my, 1 - mx], from_near.at[r], (a_x, b))

    def send_blk(r):
        step[2][r].wait_recv()
        add(r, my, mx, from_near[r])
        columns = pl.ds(pl.multiple_of(turned(b, r) * block, 128), block)
        for q in (3, 2, 1):
            to = turned(b, q)
            piece = pl.ds(pl.multiple_of(to * rows, 16), rows)
            step[3][r, q] = send(
                sums.at[r, core, my, mx, piece], from_blk.at[q - 1, :, columns], (a, to)
            )
        kept = sums[r, core, my, mx, pl.ds(pl.multiple_of(b * rows, 16), rows)]
        hidden[:, columns] += kept.astype(jnp.float32)

    for r, n in ((0, 0), (1, 1), (3, 2), (2, 3)):
        weighted(r)
        send_core(r)
        if n >= 1:
            send_far((0, 1, 3)[n - 1])
    send_near(0)
    send_far(2)
    send_near(1)
    send_blk(0)
    send_near(3)
    send_blk(1)
    send_near(2)
    send_blk(3)
    send_blk(2)
    for copy in step[3].values():
        copy.wait_recv()
    mixed = hidden[...] + (
        from_blk[0].astype(jnp.float32)
        + from_blk[1].astype(jnp.float32)
        + from_blk[2].astype(jnp.float32)
    )
    out_ref[...] = rms_scale(mixed, gain2_ref[...].reshape(1, width)).astype(jnp.bfloat16)
    for copy in started:
        copy.wait_send()


def whole_slot_plan(
    attn_out,
    resid,
    w_o,
    norm1_gain,
    router_w,
    route_slot,
    slot_expert,
    keep,
    w_gate,
    w_up,
    w_down,
    norm2_gain,
):
    rows, width = resid.shape
    slot_dev, block, ff = w_gate.shape
    sub = slot_dev // 4
    slots = slot_expert.shape[0]
    tile = 4 * rows
    copies = 3 + 6 * sub + 12 + 16 + 4 + 3 + 12 + 12
    bf16 = jnp.bfloat16
    macs = 32 * rows * sub * ff * width * 3
    return pl.pallas_call(
        expert_kernel,
        out_shape=jax.ShapeDtypeStruct((rows, width), bf16),
        in_specs=[pl.BlockSpec(memory_space=pltpu.VMEM)] * 8
        + [pl.BlockSpec(memory_space=pl.ANY)] * 4,
        out_specs=pl.BlockSpec(memory_space=pltpu.VMEM),
        scratch_shapes=[
            pltpu.VMEM((rows, width), jnp.float32),
            pltpu.VMEM((32, rows, width + 2 * slots), bf16),
            pltpu.VMEM((sub, width, ff), bf16),
            pltpu.VMEM((sub, width, ff), bf16),
            pltpu.VMEM((4, sub, block, ff), bf16),
            pltpu.VMEM((8, tile, sub * ff), bf16),
            pltpu.VMEM((4, 2, 2, 2, tile, block), bf16),
            pltpu.VMEM((4, 2, 2, tile, block), bf16),
            pltpu.VMEM((4, 2, tile, block), bf16),
            pltpu.VMEM((4, tile, block), bf16),
            pltpu.VMEM((3, rows, width), bf16),
            pltpu.SemaphoreType.DMA((copies,)),
            pltpu.SemaphoreType.DMA((copies,)),
            pltpu.SemaphoreType.DMA((9,)),
        ],
        compiler_params=pltpu.CompilerParams(
            collective_id=0, has_side_effects=True, vmem_limit_bytes=63 * 1024 * 1024
        ),
        cost_estimate=pl.CostEstimate(
            flops=2 * macs, bytes_accessed=3 * slot_dev * block * ff * 2, transcendentals=0
        ),
    )(
        attn_out,
        resid,
        norm1_gain,
        norm2_gain,
        router_w.T,
        route_slot.T,
        slot_expert.reshape(1, slots),
        keep.reshape(1, rows),
        w_o,
        w_gate,
        w_up,
        w_down,
    )


def solution(mesh):
    placed = (
        P(("tok", "blk"), None),
        P(("tok", "blk"), None),
        P(),
        P(),
        P(),
        P(("tok", "blk"), None),
        P(),
        P(("tok", "blk")),
        P("tok", "blk", None),
        P("tok", "blk", None),
        P("tok", "blk", None),
        P(),
    )
    groups, blocks = mesh.shape["tok"], mesh.shape["blk"]

    def layer(*args):
        slot_dev = args[8].shape[0] // groups
        rows, width = args[1].shape[0] // (groups * blocks), args[1].shape[1]
        fits = slot_dev == 8 and args[8].shape[2] == 4 * rows and width == 12 * rows
        cube = groups == 8 and blocks == 4 and fits and args[2].shape == (width, width)
        plan = whole_slot_plan if cube else body
        return jax.shard_map(
            plan,
            mesh=mesh,
            in_specs=placed,
            out_specs=P(("tok", "blk"), None),
            check_vma=False,
        )(*args)

    return layer
```
